256 devices in a mesh: dp: 64 (over z, x_hi, y), tensor: 4 (over x_lo, core).
Axes of the slice: x: 4 (x_hi: 2, x_lo: 2; x = x_hi * 2 + x_lo), y: 4, z: 8, core: 2. Of those that a mesh axis runs over, the one named last changes fastest.
Arguments:
- cotangent: bfloat16 [32768, 4608], P(('dp', 'tensor')), may hold values from -24 to 24
- attn_saved: bfloat16 [32768, 2048], P('dp', 'tensor'), may hold values from -6 to 6
- attn_next: bfloat16 [32768, 2048], P('dp', 'tensor'), may hold values from -6 to 6
- weight: bfloat16 [4608, 2048], P('dp', 'tensor'), may hold values from -0.125 to 0.125
- moment1: float32 [4608, 2048], P('dp', 'tensor'), may hold values from -6 to 6
- moment2: float32 [4608, 2048], P('dp', 'tensor'), may hold values from 0.1 to 10
Outputs:
- grad_attn: bfloat16 [32768, 2048], P('dp', 'tensor')
- new_weight: bfloat16 [4608, 2048], P('dp', 'tensor')
- new_moment1: float32 [4608, 2048], P('dp', 'tensor')
- new_moment2: float32 [4608, 2048], P('dp', 'tensor')
- next_out: bfloat16 [32768, 4608], P(('dp', 'tensor'))
The draws below stay inside these ranges and needn't reach their ends.
All inputs are finite; a program needn't handle non-finite values.
Results may differ from the reference program's by a relative error of at most 0.013.
Values may be sent and summed in bfloat16 or wider, within the bound.
A program may use at most 128 MiB of HBM per device.

```python
import math
import jax
import jax.numpy as jnp
from jax import lax

D = 4608
HQ = 2048
TOKENS = 32768
N_TENSOR = 4


def spiked(array, key, source, target, blocks, factor):
    owner, partner = [(jnp.arange(array.shape[position]) // (array.shape[position] // blocks)).reshape([-1 if axis == position else 1 for axis in range(array.ndim)]) for position in (source, target)]
    chosen = jax.random.permutation(key, blocks)[partner]
    strong = (owner == chosen) | (owner == (partner + blocks // 2) % blocks)
    return jnp.where(strong, factor * array, array)


def level_of(own_key, extent, shards, smallest, high):
    level, own = 1.0, jax.random.fold_in(own_key, 6)
    for axis_at, parts in shards:
        draws = jnp.exp(jax.random.uniform(jax.random.fold_in(own, axis_at), (parts,), jnp.float32, smallest / len(shards), high / len(shards)))
        level = level * jnp.repeat(draws, extent[axis_at] // parts).reshape([-1 if axis == axis_at else 1 for axis in range(len(extent))])
    return level


def gaussian(own_key, extent, width, limit, pieces=(), kind=jnp.bfloat16):
    entries = width * jax.random.normal(own_key, extent, jnp.float32)
    if pieces:
        entries = entries * level_of(own_key, extent, pieces, -0.22, 0.18)
    return jnp.clip(entries, -limit, limit).astype(kind)


def noise_with(own_key, dims, deviation, bound, cuts, heavy, held_as=jnp.bfloat16):
    result = deviation * jax.random.normal(own_key, dims, jnp.float32)
    if cuts:
        result = result * level_of(own_key, dims, cuts, -0.22, 0.18)
    return jnp.clip(spiked(result, jax.random.fold_in(own_key, 3), *heavy), -bound, bound).astype(held_as)


def setup_inputs(seed: int = 0) -> dict:
    splits = jax.random.split(jax.random.key(seed), 7)
    cotangent = noise_with(splits[0], (TOKENS, D), 1.0, 24.0, ((0, 256),), (0, 1, 256, 6.0))
    attn_saved = gaussian(splits[1], (TOKENS, HQ), 1.0, 6.0, ((0, 64), (1, 4)))
    attn_next = gaussian(splits[2], (TOKENS, HQ), 1.0, 6.0, ((0, 64), (1, 4)))
    weight = gaussian(splits[3], (D, HQ), HQ ** -0.5, 0.125, ((0, 64), (1, 4)))
    moment1 = gaussian(splits[4], (D, HQ), 1.0, 6.0, ((0, 64), (1, 4)), jnp.float32)
    moment2 = jnp.clip(jnp.exp(math.log(10.0) - 4.6051702 * jax.random.uniform(splits[5], (D, HQ), jnp.float32) ** level_of(splits[5], (D, HQ), ((0, 64), (1, 4)), -0.2, 0.2)), 0.1, 10.0)
    return dict(cotangent=cotangent, attn_saved=attn_saved, attn_next=attn_next, weight=weight, moment1=moment1, moment2=moment2)


first_decay = 0.9
second_decay = 0.95
first_fix = 1.0 - 0.9 ** 10
second_fix = 1.0 - 0.95 ** 10
learning_rate = 0.002
weight_decay = 0.1
epsilon = 1e-08

def reference(cotangent, attn_saved, attn_next, weight, moment1, moment2):
    gradient = lax.dot_general(cotangent, attn_saved, (((0,), (0,)), ((), ())), preferred_element_type=jnp.float32)
    gradient = gradient * (1.0 / math.sqrt(TOKENS))
    grad_attn = jnp.dot(cotangent, weight, preferred_element_type=jnp.float32).astype(jnp.bfloat16)
    new_moment1 = first_decay * moment1 + (1.0 - first_decay) * gradient
    new_moment2 = second_decay * moment2 + (1.0 - second_decay) * gradient * gradient
    update = new_moment1 / first_fix / (jnp.sqrt(new_moment2 / second_fix) + epsilon)
    new_weight = (weight.astype(jnp.float32) * (1.0 - learning_rate * weight_decay) - learning_rate * update).astype(jnp.bfloat16)
    group_width = HQ // N_TENSOR
    next_out = jnp.zeros((TOKENS, D), jnp.float32)
    for head_group in range(N_TENSOR):
        lower = head_group * group_width
        product = lax.dot_general(attn_next[:, lower:lower + group_width], new_weight[:, lower:lower + group_width], (((1,), (1,)), ((), ())), preferred_element_type=jnp.float32)
        rounded = lax.optimization_barrier(product.astype(jnp.bfloat16))
        next_out = next_out + rounded.astype(jnp.float32)
    return (grad_attn, new_weight, new_moment1, new_moment2, next_out.astype(jnp.bfloat16))
```

```python
import math

import jax
import jax.numpy as jnp
from jax import lax
from jax.experimental import pallas as pl
from jax.experimental.pallas import tpu as pltpu
from jax.sharding import PartitionSpec as P

F32, BF16 = jnp.float32, jnp.bfloat16
MESH = pl.DeviceIdType.MESH

first_decay = 0.9
second_decay = 0.95
first_fix = 1.0 - 0.9**10
second_fix = 1.0 - 0.95**10
learning_rate = 0.002
weight_decay = 0.1
epsilon = 1e-08

TOKENS = 32768
OWN = 72
BLK = 2 * OWN
QR = 8 * BLK
N_COPY = 128


def nt(a, b):
    return lax.dot_general(a, b, (((1,), (1,)), ((), ())), preferred_element_type=F32)


def stack(v):
    return jnp.concatenate([v[:, :256], v[:, 256:]], axis=0).astype(BF16)


def unstack(v):
    v = v.astype(F32)
    return jnp.concatenate([v[:OWN], v[OWN:]], axis=1)


def kernel(
    c_ref, a_ref, n_ref, w_ref, m1_ref, m2_ref,
    ga_ref, nw_ref, nm1_ref, nm2_ref, out_ref,
    t32, q, ct, ab, nb, nr, g32, rs_s, rs_r, gx_s, gx_r,
    w_s, w_r, wb, wt, w2_s, w2_r, wb2, gs, gr,
    os_, ok, orv, xs, xk, xr, fy, yr,
    ssem, rsem,
):
    dp, t = lax.axis_index("dp"), lax.axis_index("tensor")
    z, xh, y = lax.div(dp, 8), lax.rem(lax.div(dp, 4), 2), lax.rem(dp, 4)
    xl, c = lax.div(t, 2), lax.rem(t, 2)

    def at(dz=0, dy=0, fxh=False, fxl=False, fc=False):
        z2, y2 = lax.rem(z + dz + 8, 8), lax.rem(y + dy + 4, 4)
        xh2 = 1 - xh if fxh else xh
        xl2 = 1 - xl if fxl else xl
        c2 = 1 - c if fc else c
        return (z2 * 8 + xh2 * 4 + y2, xl2 * 2 + c2)

    copies = []

    def send(src, dst, device):
        i = len(copies)
        copy = pltpu.make_async_remote_copy(
            src_ref=src, dst_ref=dst, send_sem=ssem.at[i], recv_sem=rsem.at[i],
            device_id=device, device_id_type=MESH,
        )
        copy.start()
        copies.append(copy)
        return copy

    def zz(d):
        return lax.rem(z + d + 8, 8)

    def yy(d):
        return lax.rem(y + d + 4, 4)

    def rows(zb, n=BLK):
        return pl.ds(pl.multiple_of(zb * n, 16), n)

    barrier = pltpu.get_barrier_semaphore()
    partners = [at(dz=1), at(dz=-1), at(dy=1), at(dy=2), at(dy=3), at(fxh=True), at(fxl=True), at(fc=True)]
    for p in partners:
        pl.semaphore_signal(barrier, inc=1, device_id=p, device_id_type=MESH)

    def turn(i, _):
        col = pl.multiple_of(i * 1152, 128)
        for j in range(9):
            t32[j * 128 : (j + 1) * 128, :] = c_ref[:, pl.ds(col + j * 128, 128)].astype(F32).T
        for b in range(2):
            for k in range(4):
                lo = b * 576 + k * OWN
                v = jnp.concatenate([t32[lo : lo + OWN, :], t32[lo + 288 : lo + 288 + OWN, :]], axis=0)
                q[k, rows(2 * i + b), :] = v.astype(BF16)
        return 0

    lax.fori_loop(0, 4, turn, 0)
    ct[y, t] = q[y]
    ab[y] = a_ref[...]
    w_s[...] = stack(w_ref[...].astype(F32))
    pl.semaphore_wait(barrier, len(partners))

    def gather_z(buf):
        sent = {}

        def hop(d, s, k):
            src = zz(-(k - 1)) if d == 0 else zz(k - 1)
            if k > 1:
                sent[d, s, k - 1].wait_recv()
            sent[d, s, k] = send(buf.at[s, rows(src)], buf.at[s, rows(src)], at(dz=1 if d == 0 else -1))

        def step(k):
            for s in range(2):
                for d in range(2):
                    if k < 4 or s == d:
                        hop(d, s, k)
                    else:
                        sent[d, s, 3].wait_recv()

        def last():
            for s in range(2):
                sent[s, s, 4].wait_recv()

        return step, last

    wx = send(w_s, w_r, at(fxh=True))
    tx = (1 - xl) * 2 + c
    x_c = {0: send(ct.at[y, t], ct.at[y, t], at(fxl=True))}
    c_c = {(0, 0): send(ct.at[y, t], ct.at[y, t], at(fc=True))}
    y_c = {}
    for d in (1, 3, 2):
        y_c[d] = send(q.at[yy(d)], ct.at[y, t], at(dy=d))
    a_c = {d: send(ab.at[y], ab.at[y], at(dy=d)) for d in (1, 3)}

    wx.wait_recv()
    mine, theirs = w_ref[...].astype(F32), unstack(w_r[...])
    both = jnp.concatenate([jnp.where(xh == 0, mine, theirs), jnp.where(xh == 0, theirs, mine)], axis=0)
    both = both.astype(BF16)
    wb[0, rows(z), :] = both[:, :256]
    wb[1, rows(z), :] = both[:, 256:]
    w_step, w_last = gather_z(wb)
    w_step(1)

    def g_block(src, zb):
        lhs = jnp.concatenate([ct[src, k, rows(zb), :] for k in range(4)], axis=1)
        return jnp.dot(lhs, ab[src], preferred_element_type=F32)

    def arrive_y(d):
        y_c[d].wait_recv()
        src = yy(-d)
        x_c[d] = send(ct.at[src, t], ct.at[src, t], at(fxl=True))
        c_c[d, 0] = send(ct.at[src, t], ct.at[src, t], at(fc=True))

    def arrive_x(d):
        x_c[d].wait_recv()
        src = yy(-d)
        c_c[d, 1] = send(ct.at[src, tx], ct.at[src, tx], at(fc=True))

    def arrive_c(d):
        c_c[d, 0].wait_recv()
        c_c[d, 1].wait_recv()

    arrive_y(1)
    arrive_y(3)
    w_step(2)
    arrive_x(0)
    arrive_c(0)

    def g_first(i, _):
        g32[rows(i), :] = g_block(y, i)
        return 0

    lax.fori_loop(0, 8, g_first, 0)
    arrive_y(2)
    w_step(3)
    arrive_x(1)
    a_c[1].wait_recv()
    a_f = {1: send(ab.at[yy(-1), pl.ds(0, 256)], ab.at[yy(-1), pl.ds(0, 256)], at(dy=1))}
    a_c[3].wait_recv()
    a_f[3] = send(ab.at[yy(1), pl.ds(256, 256)], ab.at[yy(1), pl.ds(256, 256)], at(dy=3))
    arrive_x(3)
    w_step(4)
    nb[y] = n_ref[...]
    n_c = {d: send(nb.at[y], nb.at[y], at(dy=d)) for d in (1, 3)}
    for d in (1, 3):
        arrive_c(d)

        def g_more(i, _, d=d):
            g32[rows(i), :] += g_block(yy(-d), i)
            return 0

        lax.fori_loop(0, 8, g_more, 0)
    arrive_x(2)
    arrive_c(2)
    a_f[1].wait_recv()
    a_f[3].wait_recv()

    rs = {}

    def g_end(d):
        zb = zz(d)
        g32[rows(zb), :] += g_block(yy(2), zb)

    def rs_hop(d, s, k):
        zb = zz(k if d == 0 else -k)
        acc = g32[rows(zb), s * 256 : (s + 1) * 256]
        if (d, s, k + 1) in rs:
            rs[d, s, k + 1].wait_recv()
            acc = acc + rs_r[d, s, k].astype(F32)
        rs_s[d, s, k - 1] = acc.astype(BF16)
        rs[d, s, k] = send(rs_s.at[d, s, k - 1], rs_r.at[d, s, k - 1], at(dz=1 if d == 0 else -1))

    g_end(4)
    rs_hop(0, 0, 4)
    rs_hop(1, 1, 4)
    g_end(3)
    rs_hop(0, 1, 3)
    g_end(-3)
    rs_hop(1, 0, 3)
    rs_hop(0, 0, 3)
    rs_hop(1, 1, 3)
    for k in (2, 1):
        g_end(k)
        rs_hop(0, 1, k)
        g_end(-k)
        rs_hop(1, 0, k)
        rs_hop(0, 0, k)
        rs_hop(1, 1, k)
    g_end(0)
    halves = []
    for s in range(2):
        acc = g32[rows(z), s * 256 : (s + 1) * 256]
        for d in range(2):
            rs[d, s, 1].wait_recv()
            acc = acc + rs_r[d, s, 0].astype(F32)
        halves.append(acc)
    total = jnp.concatenate(halves, axis=1)
    upper, lower = total[:OWN], total[OWN:]
    gx_s[...] = stack(jnp.where(xh == 0, lower, upper))
    gx = send(gx_s, gx_r, at(fxh=True))
    keep = jnp.where(xh == 0, upper, lower)

    n_c[1].wait_recv()
    n_f = {1: send(nb.at[yy(-1), pl.ds(0, 256)], nb.at[yy(-1), pl.ds(0, 256)], at(dy=1))}
    n_c[3].wait_recv()
    n_f[3] = send(nb.at[yy(1), pl.ds(256, 256)], nb.at[yy(1), pl.ds(256, 256)], at(dy=3))

    gx.wait_recv()
    gradient = (keep + unstack(gx_r[...])) * (1.0 / math.sqrt(TOKENS))
    new_m1 = first_decay * m1_ref[...] + (1.0 - first_decay) * gradient
    new_m2 = second_decay * m2_ref[...] + (1.0 - second_decay) * gradient * gradient
    update = new_m1 / first_fix / (jnp.sqrt(new_m2 / second_fix) + epsilon)
    new_w = w_ref[...].astype(F32) * (1.0 - learning_rate * weight_decay) - learning_rate * update
    nm1_ref[...] = new_m1
    nm2_ref[...] = new_m2
    nw_ref[...] = new_w.astype(BF16)
    w2_s[...] = stack(new_w)
    w2x = send(w2_s, w2_r, at(fxh=True))

    w_last()

    def w_turn(i, _):
        for s in range(2):
            v = wb[s, pl.ds(pl.multiple_of(i * 128, 128), 128), :].astype(F32)
            wt[s * 256 : (s + 1) * 256, pl.ds(pl.multiple_of(i * 128, 128), 128)] = v.T.astype(BF16)
        return 0

    lax.fori_loop(0, 9, w_turn, 0)

    w2x.wait_recv()
    mine, theirs = new_w, unstack(w2_r[...])
    both = jnp.concatenate([jnp.where(xh == 0, mine, theirs), jnp.where(xh == 0, theirs, mine)], axis=0)
    both = both.astype(BF16)
    wb2[0, rows(z), :] = both[:, :256]
    wb2[1, rows(z), :] = both[:, 256:]
    w2_step, w2_last = gather_z(wb2)
    w2_step(1)

    n_f[1].wait_recv()
    n_f[3].wait_recv()

    def n_turn(k, _):
        for dc in range(2):
            for dx in range(2):
                owner = (xl if dx else 1 - xl) * 2 + (c if dc else 1 - c)
                lo = pl.multiple_of(owner * 128, 128)
                to = pl.multiple_of(dx * 512 + k * 128, 128)
                nr[dc, pl.ds(to, 128), :] = nb[k, pl.ds(lo, 128), :]
        return 0

    lax.fori_loop(0, 4, n_turn, 0)

    order = (0, 1, -1, 2, -2, 3, -3, 4)
    o_c, o_x, o_y = {}, {}, []

    def out_block(i):
        zb = zz(order[i])
        lhs = jnp.concatenate([wb2[0, rows(zb), :], wb2[1, rows(zb), :]], axis=1)
        os_[zb] = nt(lhs, nr[0]).astype(BF16)
        o_c[i] = send(os_.at[zb], orv.at[zb], at(fc=True))
        ok[zb] = nt(lhs, nr[1]).astype(BF16)

    def out_core(i):
        zb = zz(order[i])
        o_c[i].wait_recv()
        v = ok[zb].astype(F32) + orv[zb].astype(F32)
        xs[zb] = v[:, :512].astype(BF16)
        o_x[i] = send(xs.at[zb], xr.at[zb], at(fxl=True))
        xk[zb] = v[:, 512:]

    def out_x(i):
        zb = zz(order[i])
        o_x[i].wait_recv()
        v = (xk[zb] + xr[zb].astype(F32)).astype(BF16)
        for k in range(4):
            fy[k, rows(zb), :] = v[:, k * 128 : (k + 1) * 128]
        for d in (1, 3, 2):
            o_y.append(send(fy.at[yy(d), rows(zb)], yr.at[y, rows(zb)], at(dy=d)))
        yr[y, rows(zb), :] = fy[y, rows(zb), :]

    def ga_part(d):
        src = yy(d)
        rhs = jnp.concatenate([ct[src, k] for k in range(4)], axis=1)
        gs[src] = jnp.dot(wt[...], rhs, preferred_element_type=F32).astype(BF16)

    ga_c = {}
    for i in range(8 + 3):
        if i in (1, 3, 5):
            w2_step(2 + (i - 1) // 2)
        if i == 7:
            w2_last()
        if i < 8:
            out_block(i)
        if 0 <= i - 1 < 8:
            out_core(i - 1)
        if i in (1, 2, 3):
            d = {1: 1, 2: 3, 3: 2}[i]
            ga_part(d)
            ga_c[d] = send(gs.at[yy(d)], gr.at[d - 1], at(dy=d))
        if 0 <= i - 3 < 8:
            out_x(i - 3)
    ga_part(0)
    acc = gs[y].astype(F32)
    for d in (1, 3, 2):
        ga_c[d].wait_recv()
        acc = acc + gr[d - 1].astype(F32)
    ga_ref[...] = acc.T.astype(BF16)

    for copy in o_y:
        copy.wait_recv()

    def back(i, _):
        for b in range(2):
            for k in range(4):
                v = yr[k, rows(2 * i + b), :].astype(F32)
                lo = b * 576 + k * OWN
                t32[lo : lo + OWN, :] = v[:OWN]
                t32[lo + 288 : lo + 288 + OWN, :] = v[OWN:]
        col = pl.multiple_of(i * 1152, 128)
        for j in range(9):
            out_ref[:, pl.ds(col + j * 128, 128)] = t32[j * 128 : (j + 1) * 128, :].T.astype(BF16)
        return 0

    lax.fori_loop(0, 4, back, 0)
    for copy in copies:
        copy.wait_send()


def local(cotangent, attn_saved, attn_next, weight, moment1, moment2):
    v = pltpu.VMEM
    scratch = [
        v((QR, 128), F32),
        v((4, QR, 128), BF16),
        v((4, 4, QR, 128), BF16),
        v((4, 512, 512), BF16),
        v((4, 512, 512), BF16),
        v((2, 1024, 512), BF16),
        v((QR, 512), F32),
        v((2, 2, 4, BLK, 256), BF16),
        v((2, 2, 4, BLK, 256), BF16),
        v((BLK, 256), BF16),
        v((BLK, 256), BF16),
        v((BLK, 256), BF16),
        v((BLK, 256), BF16),
        v((2, QR, 256), BF16),
        v((512, QR), BF16),
        v((BLK, 256), BF16),
        v((BLK, 256), BF16),
        v((2, QR, 256), BF16),
        v((4, 512, 512), BF16),
        v((3, 512, 512), BF16),
        v((8, BLK, 1024), BF16),
        v((8, BLK, 1024), BF16),
        v((8, BLK, 1024), BF16),
        v((8, BLK, 512), BF16),
        v((8, BLK, 512), F32),
        v((8, BLK, 512), BF16),
        v((4, QR, 128), BF16),
        v((4, QR, 128), BF16),
        pltpu.SemaphoreType.DMA((N_COPY,)),
        pltpu.SemaphoreType.DMA((N_COPY,)),
    ]
    vm = pl.BlockSpec(memory_space=pltpu.VMEM)
    s = jax.ShapeDtypeStruct
    return pl.pallas_call(
        kernel,
        out_shape=(
            s((512, 512), BF16),
            s((OWN, 512), BF16),
            s((OWN, 512), F32),
            s((OWN, 512), F32),
            s((128, 4608), BF16),
        ),
        in_specs=[vm] * 6,
        out_specs=(vm,) * 5,
        scratch_shapes=scratch,
        compiler_params=pltpu.CompilerParams(
            collective_id=0, has_side_effects=True, vmem_limit_bytes=60 * 2**20
        ),
        name="update",
    )(cotangent, attn_saved, attn_next, weight, moment1, moment2)


def solution(mesh):
    return jax.shard_map(
        local,
        mesh=mesh,
        in_specs=(P(("dp", "tensor"), None),) + (P("dp", "tensor"),) * 5,
        out_specs=(P("dp", "tensor"),) * 4 + (P(("dp", "tensor"), None),),
        check_vma=False,
    )
```

```python
import math

import jax
import jax.numpy as jnp
from jax import lax
from jax.experimental import pallas as pl
from jax.experimental.pallas import tpu as pltpu
from jax.sharding import PartitionSpec as P

F32, BF16 = jnp.float32, jnp.bfloat16
MESH = pl.DeviceIdType.MESH

first_decay = 0.9
second_decay = 0.95
first_fix = 1.0 - 0.9**10
second_fix = 1.0 - 0.95**10
learning_rate = 0.002
weight_decay = 0.1
epsilon = 1e-08

TOKENS = 32768
OWN = 72
BLK = 2 * OWN
QR = 8 * BLK
N_COPY = 128


def nt(a, b):
    return lax.dot_general(a, b, (((1,), (1,)), ((), ())), preferred_element_type=F32)


def stack(v):
    return jnp.concatenate([v[:, :256], v[:, 256:]], axis=0).astype(BF16)


def unstack(v):
    v = v.astype(F32)
    return jnp.concatenate([v[:OWN], v[OWN:]], axis=1)


def kernel(
    c_hbm, a_hbm, n_hbm, w_hbm, m1_hbm, m2_hbm,
    ga_ref, nw_ref, nm1_ref, nm2_ref, out_ref,
    c_ref, w_ref, m1_ref, m2_ref, t32, q, ct, ab, nb, nr, g32, rs_s, rs_r, gx_s, gx_r,
    w_s, w_r, wb, wt, w2_s, w2_r, wb2, gs, gr,
    os_, ok, orv, xs, xk, xr, fy, yr,
    ssem, rsem, lsem,
):
    dp, t = lax.axis_index("dp"), lax.axis_index("tensor")
    z, xh, y = lax.div(dp, 8), lax.rem(lax.div(dp, 4), 2), lax.rem(dp, 4)
    xl, c = lax.div(t, 2), lax.rem(t, 2)

    def at(dz=0, dy=0, fxh=False, fxl=False, fc=False):
        z2, y2 = lax.rem(z + dz + 8, 8), lax.rem(y + dy + 4, 4)
        xh2 = 1 - xh if fxh else xh
        xl2 = 1 - xl if fxl else xl
        c2 = 1 - c if fc else c
        return (z2 * 8 + xh2 * 4 + y2, xl2 * 2 + c2)

    copies = []

    def send(src, dst, device):
        i = len(copies)
        copy = pltpu.make_async_remote_copy(
            src_ref=src, dst_ref=dst, send_sem=ssem.at[i], recv_sem=rsem.at[i],
            device_id=device, device_id_type=MESH,
        )
        copy.start()
        copies.append(copy)
        return copy

    def zz(d):
        return lax.rem(z + d + 8, 8)

    def yy(d):
        return lax.rem(y + d + 4, 4)

    def rows(zb, n=BLK):
        return pl.ds(pl.multiple_of(zb * n, 16), n)

    loads = [
        pltpu.make_async_copy(src, dst, lsem.at[i])
        for i, (src, dst) in enumerate(
            ((c_hbm, c_ref), (w_hbm, w_ref), (a_hbm, ab.at[y]), (n_hbm, nb.at[y]), (m1_hbm, m1_ref), (m2_hbm, m2_ref))
        )
    ]
    for load in loads:
        load.start()
    barrier = pltpu.get_barrier_semaphore()
    partners = [at(dz=1), at(dz=-1), at(dy=1), at(dy=2), at(dy=3), at(fxh=True), at(fxl=True), at(fc=True)]
    for p in partners:
        pl.semaphore_signal(barrier, inc=1, device_id=p, device_id_type=MESH)

    def turn(i, _):
        col = pl.multiple_of(i * 1152, 128)
        for j in range(9):
            t32[j * 128 : (j + 1) * 128, :] = c_ref[:, pl.ds(col + j * 128, 128)].astype(F32).T
        for b in range(2):
            for k in range(4):
                lo = b * 576 + k * OWN
                v = jnp.concatenate([t32[lo : lo + OWN, :], t32[lo + 288 : lo + 288 + OWN, :]], axis=0)
                q[k, rows(2 * i + b), :] = v.astype(BF16)
        return 0

    loads[0].wait()
    lax.fori_loop(0, 4, turn, 0)
    ct[y, t] = q[y]
    loads[1].wait()
    w_s[...] = stack(w_ref[...].astype(F32))
    pl.semaphore_wait(barrier, len(partners))

    def gather_z(buf):
        sent = {}

        def hop(d, s, k):
            src = zz(-(k - 1)) if d == 0 else zz(k - 1)
            if k > 1:
                sent[d, s, k - 1].wait_recv()
            sent[d, s, k] = send(buf.at[s, rows(src)], buf.at[s, rows(src)], at(dz=1 if d == 0 else -1))

        def step(k):
            for s in range(2):
                for d in range(2):
                    if k < 4 or s == d:
                        hop(d, s, k)
                    else:
                        sent[d, s, 3].wait_recv()

        def last():
            for s in range(2):
                sent[s, s, 4].wait_recv()

        return step, last

    tx = (1 - xl) * 2 + c
    x_c, c_c, y_c = {}, {}, {}

    def c_on(d):
        src = yy(-d)
        if d:
            y_c[d].wait_recv()
        x_c[d] = send(ct.at[src, t], ct.at[src, t], at(fxl=True))
        c_c[d, 0] = send(ct.at[src, t], ct.at[src, t], at(fc=True))

    def c_y(d):
        y_c[d] = send(q.at[yy(d)], ct.at[y, t], at(dy=d))

    def c_core(d):
        x_c[d].wait_recv()
        src = yy(-d)
        c_c[d, 1] = send(ct.at[src, tx], ct.at[src, tx], at(fc=True))

    def c_all(d):
        c_c[d, 0].wait_recv()
        c_c[d, 1].wait_recv()

    def over_y(buf):
        first, rest, then = {}, {}, {}
        low = {1: 0, 3: 256}

        def one():
            for d in (1, 3):
                part = buf.at[y, pl.ds(low[d], 256)]
                first[d] = send(part, part, at(dy=d))

        def one_more():
            for d in (1, 3):
                part = buf.at[y, pl.ds(256 - low[d], 256)]
                rest[d] = send(part, part, at(dy=d))

        def two():
            for d in (1, 3):
                first[d].wait_recv()
                part = buf.at[yy(-d), pl.ds(low[d], 256)]
                then[d] = send(part, part, at(dy=d))

        def last():
            for d in (1, 3):
                rest[d].wait_recv()
                then[d].wait_recv()

        return one, one_more, two, last

    a_one, a_more, a_two, a_last = over_y(ab)
    n_one, n_more, n_two, n_last = over_y(nb)

    c_y(1)
    c_y(3)
    c_on(0)
    wx = send(w_s, w_r, at(fxh=True))

    def both_x(mine, theirs):
        v = jnp.concatenate([jnp.where(xh == 0, mine, theirs), jnp.where(xh == 0, theirs, mine)], axis=0)
        return v.astype(BF16)

    wx.wait_recv()
    v = both_x(w_ref[...].astype(F32), unstack(w_r[...]))
    wb[0, rows(z), :] = v[:, :256]
    wb[1, rows(z), :] = v[:, 256:]
    w_step, w_last = gather_z(wb)
    w_step(1)

    def g_block(src, zb):
        lhs = jnp.concatenate([ct[src, k, rows(zb), :] for k in range(4)], axis=1)
        return jnp.dot(lhs, ab[src], preferred_element_type=F32)

    def g_part(d):
        def body(i, _):
            v = g_block(yy(-d), i)
            g32[rows(i), :] = v if d == 0 else g32[rows(i), :] + v
            return 0

        lax.fori_loop(0, 8, body, 0)

    c_on(1)
    c_on(3)
    c_y(2)
    w_step(2)
    c_core(0)
    c_all(0)
    loads[2].wait()
    a_one()
    g_part(0)
    c_on(2)
    a_more()
    w_step(3)
    a_two()
    c_core(1)
    c_core(3)
    w_step(4)

    def w_turn(i, _):
        for s in range(2):
            v = wb[s, pl.ds(pl.multiple_of(i * 128, 128), 128), :].astype(F32)
            wt[s * 256 : (s + 1) * 256, pl.ds(pl.multiple_of(i * 128, 128), 128)] = v.T.astype(BF16)
        return 0

    c_all(1)
    a_last()
    loads[3].wait()
    n_one()
    g_part(1)
    c_core(2)
    c_all(3)
    g_part(3)
    c_all(2)
    n_more()

    rs, ga_c = {}, {}

    def g_end(d):
        zb = zz(d)
        g32[rows(zb), :] += g_block(yy(2), zb)

    def rs_hop(d, s, k):
        zb = zz(k if d == 0 else -k)
        acc = g32[rows(zb), s * 256 : (s + 1) * 256]
        if (d, s, k + 1) in rs:
            rs[d, s, k + 1].wait_recv()
            acc = acc + rs_r[d, s, k].astype(F32)
        rs_s[d, s, k - 1] = acc.astype(BF16)
        rs[d, s, k] = send(rs_s.at[d, s, k - 1], rs_r.at[d, s, k - 1], at(dz=1 if d == 0 else -1))

    def ga_part(d):
        src = yy(d)
        rhs = jnp.concatenate([ct[src, k] for k in range(4)], axis=1)
        gs[src] = jnp.dot(wt[...], rhs, preferred_element_type=F32).astype(BF16)

    def ga_send(d):
        ga_c[d] = send(gs.at[yy(d)], gr.at[d - 1], at(dy=d))

    g_end(4)
    rs_hop(0, 0, 4)
    rs_hop(1, 1, 4)
    g_end(3)
    rs_hop(0, 1, 3)
    g_end(-3)
    rs_hop(1, 0, 3)
    g_end(2)
    g_end(-2)
    w_last()
    lax.fori_loop(0, 9, w_turn, 0)
    rs_hop(0, 0, 3)
    rs_hop(1, 1, 3)
    for k in (2, 1):
        if k == 1:
            ga_part(3)
        rs_hop(0, 1, k)
        rs_hop(1, 0, k)
        if k == 2:
            g_end(1)
            g_end(-1)
            g_end(0)
            ga_part(1)
        rs_hop(0, 0, k)
        rs_hop(1, 1, k)
    ga_part(2)
    halves = []
    for s in range(2):
        acc = g32[rows(z), s * 256 : (s + 1) * 256]
        for d in range(2):
            rs[d, s, 1].wait_recv()
            acc = acc + rs_r[d, s, 0].astype(F32)
        halves.append(acc)
    total = jnp.concatenate(halves, axis=1)
    upper, lower = total[:OWN], total[OWN:]
    gx_s[...] = stack(jnp.where(xh == 0, lower, upper))
    gx = send(gx_s, gx_r, at(fxh=True))
    keep = jnp.where(xh == 0, upper, lower)

    n_two()
    ga_send(1)
    ga_send(3)
    ga_part(0)

    gx.wait_recv()
    loads[4].wait()
    loads[5].wait()
    gradient = (keep + unstack(gx_r[...])) * (1.0 / math.sqrt(TOKENS))
    new_m1 = first_decay * m1_ref[...] + (1.0 - first_decay) * gradient
    new_m2 = second_decay * m2_ref[...] + (1.0 - second_decay) * gradient * gradient
    update = new_m1 / first_fix / (jnp.sqrt(new_m2 / second_fix) + epsilon)
    new_w = w_ref[...].astype(F32) * (1.0 - learning_rate * weight_decay) - learning_rate * update
    w2_s[...] = stack(new_w)
    w2x = send(w2_s, w2_r, at(fxh=True))
    nm1_ref[...] = new_m1
    nm2_ref[...] = new_m2
    nw_ref[...] = new_w.astype(BF16)

    n_last()
    ga_send(2)

    def n_turn(k, _):
        for dc in range(2):
            for dx in range(2):
                owner = (xl if dx else 1 - xl) * 2 + (c if dc else 1 - c)
                lo = pl.multiple_of(owner * 128, 128)
                to = pl.multiple_of(dx * 512 + k * 128, 128)
                nr[dc, pl.ds(to, 128), :] = nb[k, pl.ds(lo, 128), :]
        return 0

    lax.fori_loop(0, 4, n_turn, 0)

    w2x.wait_recv()
    v = both_x(new_w, unstack(w2_r[...]))
    wb2[0, rows(z), :] = v[:, :256]
    wb2[1, rows(z), :] = v[:, 256:]
    w2_step, w2_last = gather_z(wb2)
    w2_step(1)

    order = (0, 1, -1, 2, -2, 3, -3, 4)
    o_c, o_x, o_y = {}, {}, []

    def out_block(i):
        zb = zz(order[i])
        lhs = jnp.concatenate([wb2[0, rows(zb), :], wb2[1, rows(zb), :]], axis=1)
        os_[zb] = nt(lhs, nr[0]).astype(BF16)
        o_c[i] = send(os_.at[zb], orv.at[zb], at(fc=True))
        ok[zb] = nt(lhs, nr[1]).astype(BF16)

    def out_core(i):
        zb = zz(order[i])
        o_c[i].wait_recv()
        v = ok[zb].astype(F32) + orv[zb].astype(F32)
        xs[zb] = v[:, :512].astype(BF16)
        o_x[i] = send(xs.at[zb], xr.at[zb], at(fxl=True))
        xk[zb] = v[:, 512:]

    def out_x(i):
        zb = zz(order[i])
        o_x[i].wait_recv()
        v = (xk[zb] + xr[zb].astype(F32)).astype(BF16)
        for k in range(4):
            fy[k, rows(zb), :] = v[:, k * 128 : (k + 1) * 128]
        for d in (1, 3, 2):
            o_y.append(send(fy.at[yy(d), rows(zb)], yr.at[y, rows(zb)], at(dy=d)))
        yr[y, rows(zb), :] = fy[y, rows(zb), :]

    for i in range(8 + 3):
        if i in (1, 3, 5):
            w2_step(2 + (i - 1) // 2)
        if i == 7:
            w2_last()
        if i < 8:
            out_block(i)
        if 0 <= i - 1 < 8:
            out_core(i - 1)
        if 0 <= i - 3 < 8:
            out_x(i - 3)
    acc = gs[y].astype(F32)
    for d in (1, 3, 2):
        ga_c[d].wait_recv()
        acc = acc + gr[d - 1].astype(F32)
    ga_ref[...] = acc.T.astype(BF16)

    for copy in o_y:
        copy.wait_recv()

    def back(i, _):
        for b in range(2):
            for k in range(4):
                v = yr[k, rows(2 * i + b), :].astype(F32)
                lo = b * 576 + k * OWN
                t32[lo : lo + OWN, :] = v[:OWN]
                t32[lo + 288 : lo + 288 + OWN, :] = v[OWN:]
        col = pl.multiple_of(i * 1152, 128)
        for j in range(9):
            out_ref[:, pl.ds(col + j * 128, 128)] = t32[j * 128 : (j + 1) * 128, :].T.astype(BF16)
        return 0

    lax.fori_loop(0, 4, back, 0)
    for copy in copies:
        copy.wait_send()


def put(*refs):
    copies = [pltpu.make_async_copy(refs[i], refs[5 + i], refs[10].at[i]) for i in range(5)]
    for copy in copies:
        copy.start()
    for copy in copies:
        copy.wait()


def local(cotangent, attn_saved, attn_next, weight, moment1, moment2):
    v = pltpu.VMEM
    scratch = [
        v((128, 4608), BF16),
        v((OWN, 512), BF16),
        v((OWN, 512), F32),
        v((OWN, 512), F32),
        v((QR, 128), F32),
        v((4, QR, 128), BF16),
        v((4, 4, QR, 128), BF16),
        v((4, 512, 512), BF16),
        v((4, 512, 512), BF16),
        v((2, 1024, 512), BF16),
        v((QR, 512), F32),
        v((2, 2, 4, BLK, 256), BF16),
        v((2, 2, 4, BLK, 256), BF16),
        v((BLK, 256), BF16),
        v((BLK, 256), BF16),
        v((BLK, 256), BF16),
        v((BLK, 256), BF16),
        v((2, QR, 256), BF16),
        v((512, QR), BF16),
        v((BLK, 256), BF16),
        v((BLK, 256), BF16),
        v((2, QR, 256), BF16),
        v((4, 512, 512), BF16),
        v((3, 512, 512), BF16),
        v((8, BLK, 1024), BF16),
        v((8, BLK, 1024), BF16),
        v((8, BLK, 1024), BF16),
        v((8, BLK, 512), BF16),
        v((8, BLK, 512), F32),
        v((8, BLK, 512), BF16),
        v((4, QR, 128), BF16),
        v((4, QR, 128), BF16),
        pltpu.SemaphoreType.DMA((N_COPY,)),
        pltpu.SemaphoreType.DMA((N_COPY,)),
        pltpu.SemaphoreType.DMA((6,)),
    ]
    vm = pl.BlockSpec(memory_space=pltpu.VMEM)
    s = jax.ShapeDtypeStruct
    shapes = (
        s((512, 512), BF16),
        s((OWN, 512), BF16),
        s((OWN, 512), F32),
        s((OWN, 512), F32),
        s((128, 4608), BF16),
    )
    results = pl.pallas_call(
        kernel,
        out_shape=tuple(v(x.shape, x.dtype) for x in shapes),
        in_specs=[pl.BlockSpec(memory_space=pltpu.HBM)] * 6,
        out_specs=(vm,) * 5,
        scratch_shapes=scratch,
        compiler_params=pltpu.CompilerParams(
            collective_id=0, has_side_effects=True, vmem_limit_bytes=64 * 2**20 - 2150000
        ),
        name="update",
    )(cotangent, attn_saved, attn_next, weight, moment1, moment2)
    return pl.pallas_call(
        put,
        out_shape=shapes,
        in_specs=[vm] * 5,
        out_specs=(pl.BlockSpec(memory_space=pl.ANY),) * 5,
        scratch_shapes=[pltpu.SemaphoreType.DMA((5,))],
        compiler_params=pltpu.CompilerParams(vmem_limit_bytes=4 * 2**20),
        name="put",
    )(*results)


def solution(mesh):
    return jax.shard_map(
        local,
        mesh=mesh,
        in_specs=(P(("dp", "tensor"), None),) + (P("dp", "tensor"),) * 5,
        out_specs=(P("dp", "tensor"),) * 4 + (P(("dp", "tensor"), None),),
        check_vma=False,
    )
```

```python
import math

import jax
import jax.numpy as jnp
from jax import lax
from jax.experimental import pallas as pl
from jax.experimental.pallas import tpu as pltpu
from jax.sharding import PartitionSpec as P

F32, BF16 = jnp.float32, jnp.bfloat16
MESH = pl.DeviceIdType.MESH

first_decay = 0.9
second_decay = 0.95
first_fix = 1.0 - 0.9**10
second_fix = 1.0 - 0.95**10
learning_rate = 0.002
weight_decay = 0.1
epsilon = 1e-08

TOKENS = 32768
OWN = 72
BLK = 2 * OWN
QR = 8 * BLK
N_COPY = 128


def nt(a, b):
    return lax.dot_general(a, b, (((1,), (1,)), ((), ())), preferred_element_type=F32)


def stack(v):
    return jnp.concatenate([v[:, :256], v[:, 256:]], axis=0).astype(BF16)


def unstack(v):
    v = v.astype(F32)
    return jnp.concatenate([v[:OWN], v[OWN:]], axis=1)


def kernel(
    c_hbm, a_hbm, n_hbm, w_hbm, m1_hbm, m2_hbm,
    ga_ref, nw_ref, nm1_ref, nm2_ref, out_ref,
    c_ref, w_ref, m1_ref, m2_ref, t32, q, ct, ab, nb, nr, g32, rs_s, rs_r, gx_s, gx_r,
    w_s, w_r, wb, wt, w2_s, w2_r, wb2, gs, gr,
    os_, ok, orv, xs, xk, xr, fy, yr,
    ssem, rsem, lsem,
):
    dp, t = lax.axis_index("dp"), lax.axis_index("tensor")
    z, xh, y = lax.div(dp, 8), lax.rem(lax.div(dp, 4), 2), lax.rem(dp, 4)
    xl, c = lax.div(t, 2), lax.rem(t, 2)

    def at(dz=0, dy=0, fxh=False, fxl=False, fc=False):
        z2, y2 = lax.rem(z + dz + 8, 8), lax.rem(y + dy + 4, 4)
        xh2 = 1 - xh if fxh else xh
        xl2 = 1 - xl if fxl else xl
        c2 = 1 - c if fc else c
        return (z2 * 8 + xh2 * 4 + y2, xl2 * 2 + c2)

    copies = []

    def send(src, dst, device):
        i = len(copies)
        copy = pltpu.make_async_remote_copy(
            src_ref=src, dst_ref=dst, send_sem=ssem.at[i], recv_sem=rsem.at[i],
            device_id=device, device_id_type=MESH,
        )
        copy.start()
        copies.append(copy)
        return copy

    def zz(d):
        return lax.rem(z + d + 8, 8)

    def yy(d):
        return lax.rem(y + d + 4, 4)

    def rows(zb, n=BLK):
        return pl.ds(pl.multiple_of(zb * n, 16), n)

    loads = [
        pltpu.make_async_copy(src, dst, lsem.at[i])
        for i, (src, dst) in enumerate(
            ((c_hbm, c_ref), (w_hbm, w_ref), (a_hbm, ab.at[y]), (n_hbm, nb.at[y]), (m1_hbm, m1_ref), (m2_hbm, m2_ref))
        )
    ]
    for load in loads:
        load.start()
    barrier = pltpu.get_barrier_semaphore()
    partners = [at(dz=1), at(dz=-1), at(dy=1), at(dy=2), at(dy=3), at(fxh=True), at(fxl=True), at(fc=True)]
    for p in partners:
        pl.semaphore_signal(barrier, inc=1, device_id=p, device_id_type=MESH)

    def turn(i, _):
        col = pl.multiple_of(i * 1152, 128)
        for j in range(9):
            t32[j * 128 : (j + 1) * 128, :] = c_ref[:, pl.ds(col + j * 128, 128)].astype(F32).T
        for b in range(2):
            for k in range(4):
                lo = b * 576 + k * OWN
                v = jnp.concatenate([t32[lo : lo + OWN, :], t32[lo + 288 : lo + 288 + OWN, :]], axis=0)
                q[k, rows(2 * i + b), :] = v.astype(BF16)
        return 0

    loads[0].wait()
    lax.fori_loop(0, 4, turn, 0)
    ct[y, t] = q[y]
    loads[1].wait()
    w_s[...] = stack(w_ref[...].astype(F32))
    pl.semaphore_wait(barrier, len(partners))

    def gather_z(buf):
        sent = {}

        def hop(d, s, k):
            src = zz(-(k - 1)) if d == 0 else zz(k - 1)
            if k > 1:
                sent[d, s, k - 1].wait_recv()
            sent[d, s, k] = send(buf.at[s, rows(src)], buf.at[s, rows(src)], at(dz=1 if d == 0 else -1))

        def step(k):
            for s in range(2):
                for d in range(2):
                    if k < 4 or s == d:
                        hop(d, s, k)
                    else:
                        sent[d, s, 3].wait_recv()

        def last():
            for s in range(2):
                sent[s, s, 4].wait_recv()

        return step, last

    tx = (1 - xl) * 2 + c
    x_c, c_c, y_c = {}, {}, {}

    def c_on(d):
        src = yy(-d)
        if d:
            y_c[d].wait_recv()
        x_c[d] = send(ct.at[src, t], ct.at[src, t], at(fxl=True))
        c_c[d, 0] = send(ct.at[src, t], ct.at[src, t], at(fc=True))

    def c_y(d):
        y_c[d] = send(q.at[yy(d)], ct.at[y, t], at(dy=d))

    def c_core(d):
        x_c[d].wait_recv()
        src = yy(-d)
        c_c[d, 1] = send(ct.at[src, tx], ct.at[src, tx], at(fc=True))

    def c_all(d):
        c_c[d, 0].wait_recv()
        c_c[d, 1].wait_recv()

    def over_y(buf):
        first, rest, then = {}, {}, {}
        low = {1: 0, 3: 256}

        def one():
            for d in (1, 3):
                part = buf.at[y, pl.ds(low[d], 256)]
                first[d] = send(part, part, at(dy=d))

        def one_more():
            for d in (1, 3):
                part = buf.at[y, pl.ds(256 - low[d], 256)]
                rest[d] = send(part, part, at(dy=d))

        def two():
            for d in (1, 3):
                first[d].wait_recv()
                part = buf.at[yy(-d), pl.ds(low[d], 256)]
                then[d] = send(part, part, at(dy=d))

        def last():
            for d in (1, 3):
                rest[d].wait_recv()
                then[d].wait_recv()

        return one, one_more, two, last

    a_one, a_more, a_two, a_last = over_y(ab)
    n_one, n_more, n_two, n_last = over_y(nb)

    c_on(0)
    c_y(1)
    c_y(3)
    wx = send(w_s, w_r, at(fxh=True))

    def both_x(mine, theirs):
        v = jnp.concatenate([jnp.where(xh == 0, mine, theirs), jnp.where(xh == 0, theirs, mine)], axis=0)
        return v.astype(BF16)

    wx.wait_recv()
    v = both_x(w_ref[...].astype(F32), unstack(w_r[...]))
    wb[0, rows(z), :] = v[:, :256]
    wb[1, rows(z), :] = v[:, 256:]
    w_step, w_last = gather_z(wb)
    w_step(1)

    def g_block(src, zb):
        lhs = jnp.concatenate([ct[src, k, rows(zb), :] for k in range(4)], axis=1)
        return jnp.dot(lhs, ab[src], preferred_element_type=F32)

    def g_part(d):
        def body(i, _):
            v = g_block(yy(-d), i)
            g32[rows(i), :] = v if d == 0 else g32[rows(i), :] + v
            return 0

        lax.fori_loop(0, 8, body, 0)

    c_on(1)
    c_on(3)
    c_y(2)
    w_step(2)
    c_core(0)
    c_all(0)
    loads[2].wait()
    a_one()
    g_part(0)
    c_on(2)
    a_more()
    w_step(3)
    a_two()
    c_core(1)
    c_core(3)
    w_step(4)

    def w_turn(i, _):
        for s in range(2):
            v = wb[s, pl.ds(pl.multiple_of(i * 128, 128), 128), :].astype(F32)
            wt[s * 256 : (s + 1) * 256, pl.ds(pl.multiple_of(i * 128, 128), 128)] = v.T.astype(BF16)
        return 0

    c_all(1)
    a_last()
    loads[3].wait()
    n_one()
    g_part(1)
    c_core(2)
    c_all(3)
    g_part(3)
    c_all(2)
    n_more()

    rs, ga_c = {}, {}

    def g_end(d):
        zb = zz(d)
        g32[rows(zb), :] += g_block(yy(2), zb)

    def rs_hop(d, s, k):
        zb = zz(k if d == 0 else -k)
        acc = g32[rows(zb), s * 256 : (s + 1) * 256]
        if (d, s, k + 1) in rs:
            rs[d, s, k + 1].wait_recv()
            acc = acc + rs_r[d, s, k].astype(F32)
        rs_s[d, s, k - 1] = acc.astype(BF16)
        rs[d, s, k] = send(rs_s.at[d, s, k - 1], rs_r.at[d, s, k - 1], at(dz=1 if d == 0 else -1))

    def ga_part(d):
        src = yy(d)
        rhs = jnp.concatenate([ct[src, k] for k in range(4)], axis=1)
        gs[src] = jnp.dot(wt[...], rhs, preferred_element_type=F32).astype(BF16)

    def ga_send(d):
        ga_c[d] = send(gs.at[yy(d)], gr.at[d - 1], at(dy=d))

    g_end(4)
    rs_hop(0, 0, 4)
    rs_hop(1, 1, 4)
    g_end(3)
    rs_hop(0, 1, 3)
    g_end(-3)
    rs_hop(1, 0, 3)
    g_end(2)
    g_end(-2)
    w_last()
    lax.fori_loop(0, 9, w_turn, 0)
    rs_hop(0, 0, 3)
    rs_hop(1, 1, 3)
    for k in (2, 1):
        if k == 1:
            ga_part(3)
        rs_hop(0, 1, k)
        rs_hop(1, 0, k)
        if k == 2:
            g_end(1)
            g_end(-1)
            g_end(0)
            ga_part(1)
            n_two()
        rs_hop(0, 0, k)
        rs_hop(1, 1, k)
    ga_part(2)
    halves = []
    for s in range(2):
        acc = g32[rows(z), s * 256 : (s + 1) * 256]
        for d in range(2):
            rs[d, s, 1].wait_recv()
            acc = acc + rs_r[d, s, 0].astype(F32)
        halves.append(acc)
    total = jnp.concatenate(halves, axis=1)
    upper, lower = total[:OWN], total[OWN:]
    gx_s[...] = stack(jnp.where(xh == 0, lower, upper))
    gx = send(gx_s, gx_r, at(fxh=True))
    keep = jnp.where(xh == 0, upper, lower)

    ga_send(1)
    ga_send(3)
    ga_part(0)

    gx.wait_recv()
    loads[4].wait()
    loads[5].wait()
    gradient = (keep + unstack(gx_r[...])) * (1.0 / math.sqrt(TOKENS))
    new_m1 = first_decay * m1_ref[...] + (1.0 - first_decay) * gradient
    new_m2 = second_decay * m2_ref[...] + (1.0 - second_decay) * gradient * gradient
    update = new_m1 / first_fix / (jnp.sqrt(new_m2 / second_fix) + epsilon)
    new_w = w_ref[...].astype(F32) * (1.0 - learning_rate * weight_decay) - learning_rate * update
    w2_s[...] = stack(new_w)
    w2x = send(w2_s, w2_r, at(fxh=True))
    nm1_ref[...] = new_m1
    nm2_ref[...] = new_m2
    nw_ref[...] = new_w.astype(BF16)

    n_last()
    ga_send(2)

    def n_turn(k, _):
        for dc in range(2):
            for dx in range(2):
                owner = (xl if dx else 1 - xl) * 2 + (c if dc else 1 - c)
                lo = pl.multiple_of(owner * 128, 128)
                to = pl.multiple_of(dx * 512 + k * 128, 128)
                nr[dc, pl.ds(to, 128), :] = nb[k, pl.ds(lo, 128), :]
        return 0

    lax.fori_loop(0, 4, n_turn, 0)

    w2x.wait_recv()
    v = both_x(new_w, unstack(w2_r[...]))
    wb2[0, rows(z), :] = v[:, :256]
    wb2[1, rows(z), :] = v[:, 256:]
    w2_step, w2_last = gather_z(wb2)
    w2_step(1)

    order = (0, 1, -1, 2, -2, 3, -3, 4)
    o_c, o_x, o_y = {}, {}, []

    def out_block(ids):
        zs = [zz(order[i]) for i in ids]
        lhs = [jnp.concatenate([wb2[0, rows(zb), :], wb2[1, rows(zb), :]], axis=1) for zb in zs]
        lhs = lhs[0] if len(lhs) == 1 else jnp.concatenate(lhs, axis=0)
        for dc, to in ((0, os_), (1, ok)):
            v = nt(lhs, nr[dc]).astype(BF16)
            for j, i in enumerate(ids):
                to[zs[j]] = v[j * BLK : (j + 1) * BLK]
                if dc == 0:
                    o_c[i] = send(os_.at[zs[j]], orv.at[zs[j]], at(fc=True))

    def out_core(i):
        zb = zz(order[i])
        o_c[i].wait_recv()
        v = ok[zb].astype(F32) + orv[zb].astype(F32)
        xs[zb] = v[:, :512].astype(BF16)
        o_x[i] = send(xs.at[zb], xr.at[zb], at(fxl=True))
        xk[zb] = v[:, 512:]

    def out_x(i):
        zb = zz(order[i])
        o_x[i].wait_recv()
        v = (xk[zb] + xr[zb].astype(F32)).astype(BF16)
        for k in range(4):
            fy[k, rows(zb), :] = v[:, k * 128 : (k + 1) * 128]
        for d in (1, 3, 2):
            o_y.append(send(fy.at[yy(d), rows(zb)], yr.at[y, rows(zb)], at(dy=d)))
        yr[y, rows(zb), :] = fy[y, rows(zb), :]

    for i in range(8 + 3):
        if i in (1, 3, 5):
            w2_step(2 + (i - 1) // 2)
        if i == 7:
            w2_last()
        if i < 8:
            if i in (0, 7):
                out_block((i,))
            elif i % 2:
                out_block((i, i + 1))
        if 0 <= i - 1 < 8:
            out_core(i - 1)
        if 0 <= i - 3 < 8:
            out_x(i - 3)
    acc = gs[y].astype(F32)
    for d in (1, 3, 2):
        ga_c[d].wait_recv()
        acc = acc + gr[d - 1].astype(F32)
    ga_ref[...] = acc.T.astype(BF16)

    for copy in o_y:
        copy.wait_recv()

    def back(i, _):
        for b in range(2):
            for k in range(4):
                v = yr[k, rows(2 * i + b), :].astype(F32)
                lo = b * 576 + k * OWN
                t32[lo : lo + OWN, :] = v[:OWN]
                t32[lo + 288 : lo + 288 + OWN, :] = v[OWN:]
        col = pl.multiple_of(i * 1152, 128)
        for j in range(9):
            out_ref[:, pl.ds(col + j * 128, 128)] = t32[j * 128 : (j + 1) * 128, :].T.astype(BF16)
        return 0

    lax.fori_loop(0, 4, back, 0)
    for copy in copies:
        copy.wait_send()


def put(*refs):
    copies = [pltpu.make_async_copy(refs[i], refs[5 + i], refs[10].at[i]) for i in range(5)]
    for copy in copies:
        copy.start()
    for copy in copies:
        copy.wait()


def local(cotangent, attn_saved, attn_next, weight, moment1, moment2):
    v = pltpu.VMEM
    scratch = [
        v((128, 4608), BF16),
        v((OWN, 512), BF16),
        v((OWN, 512), F32),
        v((OWN, 512), F32),
        v((QR, 128), F32),
        v((4, QR, 128), BF16),
        v((4, 4, QR, 128), BF16),
        v((4, 512, 512), BF16),
        v((4, 512, 512), BF16),
        v((2, 1024, 512), BF16),
        v((QR, 512), F32),
        v((2, 2, 4, BLK, 256), BF16),
        v((2, 2, 4, BLK, 256), BF16),
        v((BLK, 256), BF16),
        v((BLK, 256), BF16),
        v((BLK, 256), BF16),
        v((BLK, 256), BF16),
        v((2, QR, 256), BF16),
        v((512, QR), BF16),
        v((BLK, 256), BF16),
        v((BLK, 256), BF16),
        v((2, QR, 256), BF16),
        v((4, 512, 512), BF16),
        v((3, 512, 512), BF16),
        v((8, BLK, 1024), BF16),
        v((8, BLK, 1024), BF16),
        v((8, BLK, 1024), BF16),
        v((8, BLK, 512), BF16),
        v((8, BLK, 512), F32),
        v((8, BLK, 512), BF16),
        v((4, QR, 128), BF16),
        v((4, QR, 128), BF16),
        pltpu.SemaphoreType.DMA((N_COPY,)),
        pltpu.SemaphoreType.DMA((N_COPY,)),
        pltpu.SemaphoreType.DMA((6,)),
    ]
    vm = pl.BlockSpec(memory_space=pltpu.VMEM)
    s = jax.ShapeDtypeStruct
    shapes = (
        s((512, 512), BF16),
        s((OWN, 512), BF16),
        s((OWN, 512), F32),
        s((OWN, 512), F32),
        s((128, 4608), BF16),
    )
    results = pl.pallas_call(
        kernel,
        out_shape=tuple(v(x.shape, x.dtype) for x in shapes),
        in_specs=[pl.BlockSpec(memory_space=pltpu.HBM)] * 6,
        out_specs=(vm,) * 5,
        scratch_shapes=scratch,
        compiler_params=pltpu.CompilerParams(
            collective_id=0, has_side_effects=True, vmem_limit_bytes=64 * 2**20 - 2150000
        ),
        name="update",
    )(cotangent, attn_saved, attn_next, weight, moment1, moment2)
    return pl.pallas_call(
        put,
        out_shape=shapes,
        in_specs=[vm] * 5,
        out_specs=(pl.BlockSpec(memory_space=pl.ANY),) * 5,
        scratch_shapes=[pltpu.SemaphoreType.DMA((5,))],
        compiler_params=pltpu.CompilerParams(vmem_limit_bytes=4 * 2**20),
        name="put",
    )(*results)


def solution(mesh):
    return jax.shard_map(
        local,
        mesh=mesh,
        in_specs=(P(("dp", "tensor"), None),) + (P("dp", "tensor"),) * 5,
        out_specs=(P("dp", "tensor"),) * 4 + (P(("dp", "tensor"), None),),
        check_vma=False,
    )
```
